32 devices in a mesh: label: 16 (over z, y, x), fsdp: 2 (over core).
Axes of the slice: x: 2, y: 2, z: 4, core: 2. Of those that a mesh axis runs over, the one named last changes fastest.
Arguments:
- final_hidden: bfloat16 [16, 32, 3584], P('label', 'fsdp'), may hold values from -6 to 6
- norm_gain: float32 [3584], replicated, may hold values from 0.5 to 1.5
- label_weights: bfloat16 [16, 128, 3584], P('label'), may hold values from -0.09375 to 0.09375
- active_blocks: int32 [16, 16, 8], P('label', 'fsdp'), may hold values from 0 to 15, all different within a row; in each aligned block of 8 rows (0 to 7, 8 to 15, ..., all dimensions but the last counted through in order) at most 6 rows name the same one
- positives: int32 [16, 32, 8], P('label', 'fsdp'), may hold values from 0 to 1023
- gate_pre: bfloat16 [16, 32, 18944], P(None, 'fsdp', 'label'), may hold values from -6 to 6
- up_pre: bfloat16 [16, 32, 18944], P(None, 'fsdp', 'label'), may hold values from -6 to 6
- down_weight: bfloat16 [3584, 18944], P('fsdp', 'label'), may hold values from -0.046875 to 0.046875
Outputs:
- resid_grad: bfloat16 [16, 32, 3584], P('label', 'fsdp')
- down_grad: float32 [3584, 18944], P('fsdp', 'label')
- gate_grad: bfloat16 [16, 32, 18944], P(None, 'fsdp', 'label')
- up_grad: bfloat16 [16, 32, 18944], P(None, 'fsdp', 'label')
The draws below stay inside these ranges and needn't reach their ends.
Inputs may be any that keep to these rules, and one draw needn't show every extreme that they name: `active_blocks`: each query block names 8 different owners; among the 8 query blocks held by one device no owner is named more than 6 times. `positives`: A code k * 128 + j names label j of the k-th active block of the query's block.
All inputs are finite; a program needn't handle non-finite values.
Results may differ from the reference program's by a relative error of at most 0.017.
Values may be sent and summed in bfloat16 or wider, within the bound.
No kernel may reach another device: no remote copies, remote signals or barrier semaphores. Data moves between devices by JAX's collectives and lax.ppermute only.
A program may use at most 64 MiB of HBM per device.

```python
import math
import jax
import jax.numpy as jnp
import numpy as np
from jax import lax

D = 3584
FF = 18944
LBLOCK = 128
ACTIVE = 8
POS = 8
QBLOCK = 2
QDEV = 16
QBLOCKS_DEV = 8
CAP = 6
N_LABEL = 16
N_FSDP = 2


def touch_ends(array, rng, least, top_value):
    extent = array.shape
    spot = [jax.random.randint(jax.random.fold_in(rng, axis), (), 0, extent[axis]) for axis in range(len(extent))]
    array = array.at[tuple(spot)].set(least)
    longest = extent.index(max(extent))
    spot[longest] = (spot[longest] + 1) % extent[longest]
    return array.at[tuple(spot)].set(top_value)


def block_levels(stream_key, shape, cuts, least, top_value):
    gain = 1.0
    for dim, blocks in cuts:
        heights = jax.random.uniform(jax.random.fold_in(jax.random.fold_in(stream_key, 6), dim), (blocks,), jnp.float32, least / len(cuts), top_value / len(cuts))
        gain = gain * jnp.repeat(jnp.exp(heights), shape[dim] // blocks).reshape((-1,) + (1,) * (len(shape) - 1 - dim))
    return gain


def assign_block(own_key, own, number, rows, number_of, top, limit, skew):
    sequence = jax.random.permutation(own_key, number_of)
    crowded, usual = shares(number_of, rows * top, limit, skew, True), shares(number_of, rows * top, limit, skew, False)
    places = jnp.arange(number_of)

    def named(lengths, offset_by):
        used = int((lengths > 0).sum())
        fixed = max(1, used // 4)
        shifted = fixed + (places - fixed + offset_by * (used - fixed)) % max(1, number_of - fixed)
        return jnp.zeros((number_of,), jnp.int32).at[sequence[jnp.where(places < fixed, places, shifted)]].set(jnp.asarray(lengths, jnp.int32))

    lengths = jnp.where(number % 4 == 0, named(crowded, number // 4), named(usual, number - number // 4 - 1))
    mixed = jax.random.permutation(jax.random.fold_in(own, 3), number_of)
    giver, taker = mixed[0:number_of // 2 * 2:2], mixed[1:number_of // 2 * 2:2]
    room = jnp.minimum(lengths[giver] - 1, limit - lengths[taker]) // 2
    room = jnp.where((giver == sequence[0]) | (taker == sequence[0]) | (lengths[taker] == 0), 0, jnp.maximum(room, 0))
    shifted = jax.random.randint(jax.random.fold_in(own, 4), (number_of // 2,), 0, 1 << 20) % (room + 1)
    lengths = lengths.at[giver].add(-shifted).at[taker].add(shifted)
    items = jnp.searchsorted(jnp.cumsum(lengths), jnp.arange(rows * top), side="right").astype(jnp.int32)
    listing = items.reshape(top, rows).T
    listing = listing[jax.random.permutation(jax.random.fold_in(own, 1), rows)]
    offset_by = jax.random.randint(jax.random.fold_in(own, 2), (rows, 1), 0, top)
    return jnp.take_along_axis(listing, (jnp.arange(top)[None, :] + offset_by) % top, axis=1)


def shares(number_of, total, limit, lean, full):
    loads = [(1 << 20) // math.isqrt(rank ** lean) + 1 for rank in range(1, number_of + 1)]
    largest = limit if full else min(limit, max(-(-total // number_of), total * loads[0] // sum(loads)))
    least = 1 if total - largest >= number_of - 1 else 0
    given, surplus = [largest] + [least] * (number_of - 1), total - largest - least * (number_of - 1)
    while surplus > 0:
        free = [i for i in range(1, number_of) if given[i] < largest] or [i for i in range(1, number_of) if given[i] < limit]
        mass, remaining = sum([loads[i] for i in free]), surplus
        for i in free:
            addition = min(limit - given[i], max(1, remaining * loads[i] // mass), surplus)
            given[i] = given[i] + addition
            surplus = surplus - addition
    return np.array(given)


def centred(rng, dims, spread, bound, cuts=(), kind=jnp.bfloat16):
    level = block_levels(rng, dims, cuts, -0.22, 0.18) if cuts else 1.0
    array = jax.random.normal(rng, dims, jnp.float32) * spread * level
    return jnp.minimum(jnp.maximum(array, -bound), bound).astype(kind)


def setup_inputs(seed: int = 0) -> dict:
    key_of = jax.random.split(jax.random.key(seed), 9)
    final_hidden = centred(key_of[0], (N_LABEL, N_FSDP * QDEV, D), 1.0, 6.0, ((0, 16), (1, 2)))
    norm_gain = jnp.clip(1.0 + 0.1 * jax.random.normal(key_of[1], (D,), jnp.float32), 0.5, 1.5)
    label_weights = centred(key_of[2], (N_LABEL, LBLOCK, D), D ** -0.5, 0.09375, ((0, 16),))
    active_blocks_keys = jax.random.split(jax.random.fold_in(key_of[3], 1), N_LABEL * (N_FSDP * QBLOCKS_DEV) // QBLOCKS_DEV)
    active_blocks_turns = jax.random.permutation(jax.random.fold_in(key_of[3], 3), N_LABEL * (N_FSDP * QBLOCKS_DEV) // QBLOCKS_DEV)
    active_blocks = jax.vmap(lambda own, number: assign_block(jax.random.fold_in(key_of[3], 2), own, number, QBLOCKS_DEV, N_LABEL, ACTIVE, CAP, 2))(active_blocks_keys, active_blocks_turns).reshape((N_LABEL, N_FSDP * QBLOCKS_DEV, ACTIVE))
    positives = touch_ends(jax.random.randint(key_of[4], (N_LABEL, N_FSDP * QDEV, POS), 0, ACTIVE * LBLOCK), jax.random.fold_in(key_of[4], 1), 0, (ACTIVE * LBLOCK) - 1).astype(jnp.int32)
    gate_pre = centred(key_of[5], (N_LABEL, N_FSDP * QDEV, FF), 1.0, 6.0, ((1, 2), (2, 16)))
    up_pre = centred(key_of[6], (N_LABEL, N_FSDP * QDEV, FF), 1.0, 6.0, ((1, 2), (2, 16)))
    down_weight = centred(key_of[7], (D, FF), FF ** -0.5, 0.046875, ((0, 2), (1, 16)))
    return dict(final_hidden=final_hidden, norm_gain=norm_gain, label_weights=label_weights, active_blocks=active_blocks, positives=positives, gate_pre=gate_pre, up_pre=up_pre, down_weight=down_weight)


norm_epsilon = 1e-06

def reference(final_hidden, norm_gain, label_weights, active_blocks, positives, gate_pre, up_pre, down_weight):
    query_total = final_hidden.shape[0] * final_hidden.shape[1]
    hidden_rows = final_hidden.reshape(query_total, D).astype(jnp.float32)
    inverse_rms = lax.rsqrt(lax.optimization_barrier(jnp.mean(hidden_rows * hidden_rows, axis=1, keepdims=True)) + norm_epsilon)
    normed = hidden_rows * inverse_rms
    embedded = (normed * norm_gain).astype(jnp.bfloat16)
    block_total = query_total // QBLOCK
    embed_blocks = embedded.reshape(block_total, QBLOCK, D)
    owner_table = active_blocks.reshape(block_total, ACTIVE)
    code_table = positives.reshape(block_total, QBLOCK, POS)
    targets = (jnp.arange(ACTIVE, dtype=jnp.int32)[:, None] * LBLOCK + jnp.arange(LBLOCK, dtype=jnp.int32)[None, :]).astype(jnp.int32)

    def one_block(item):
        block_embed, block_owners, block_codes = item
        weights_here = label_weights[block_owners].astype(jnp.float32)
        scores = jnp.einsum('qd,kld->kql', block_embed.astype(jnp.float32), weights_here)
        positive = jnp.any(block_codes[None, :, :, None] == targets[:, None, None, :], axis=2)
        target_sign = jnp.where(positive, 1.0, -1.0).astype(jnp.float32)
        margin = jnp.maximum(1.0 - target_sign * scores, 0.0)
        slope = (-2.0 * target_sign * margin).astype(jnp.bfloat16)
        slope = lax.optimization_barrier(slope).astype(jnp.float32)
        parts = jnp.einsum('kql,kld->kqd', slope, weights_here).astype(jnp.bfloat16)
        parts = lax.optimization_barrier(parts).astype(jnp.float32)
        return lax.optimization_barrier(jnp.sum(parts, axis=0))
    embed_grad = lax.map(one_block, (embed_blocks, owner_table, code_table)).reshape(query_total, D)
    scaled = norm_gain * embed_grad
    resid = inverse_rms * (scaled - normed * lax.optimization_barrier(jnp.mean(normed * scaled, axis=1, keepdims=True)))
    resid_bf = resid.astype(jnp.bfloat16)
    resid_grad = resid_bf.reshape(final_hidden.shape)
    gate_full = gate_pre.astype(jnp.float32)
    up_full = up_pre.astype(jnp.float32)
    sigma = jax.nn.sigmoid(gate_full)
    hidden_act = (gate_full * sigma * up_full).astype(jnp.bfloat16)
    label_count = gate_pre.shape[0]
    group_count = final_hidden.shape[1] // QDEV
    resid_groups = jnp.transpose(resid_bf.reshape(label_count, group_count, QDEV, D), (1, 0, 2, 3)).reshape(group_count, label_count * QDEV, D)
    hidden_groups = jnp.transpose(hidden_act.reshape(label_count, group_count, QDEV, FF), (1, 0, 2, 3)).reshape(group_count, label_count * QDEV, FF)

    def add_group(total, pair):
        group_resid, group_hidden = pair
        term = jnp.dot(group_resid.T, group_hidden, preferred_element_type=jnp.float32).astype(jnp.bfloat16)
        term = lax.optimization_barrier(term).astype(jnp.float32)
        return (total + term, None)
    down_grad, _ = lax.scan(add_group, jnp.zeros((D, FF), jnp.float32), (resid_groups, hidden_groups))
    hidden_grad = jnp.dot(resid_bf, down_weight, preferred_element_type=jnp.float32).reshape(gate_pre.shape)
    up_grad = (hidden_grad * gate_full * sigma).astype(jnp.bfloat16)
    gate_grad = (hidden_grad * up_full * sigma * (1.0 + gate_full * (1.0 - sigma))).astype(jnp.bfloat16)
    return (resid_grad, down_grad, gate_grad, up_grad)
```

```python
import jax
import jax.numpy as jnp
from jax import lax
from jax.sharding import PartitionSpec as P

ACTIVE = 8
QBLOCK = 2
PLANE = 4
META = 128

norm_epsilon = 1e-06


def shards(
    final_hidden, norm_gain, label_weights, active_blocks, positives, gate_pre, up_pre, down_weight
):
    owners = lax.axis_size("label")
    groups = lax.axis_size("fsdp")
    depth = owners // PLANE
    here = lax.axis_index("label")
    core = lax.axis_index("fsdp")
    label_rows = label_weights[0]
    block_labels, width = label_rows.shape
    share = block_labels // groups
    half = width // 2

    def across(array, mask):
        return lax.ppermute(array, "label", [(i, i ^ mask) for i in range(owners)])

    def along(array, step):
        return lax.ppermute(
            array, "label", [(i, (i + PLANE * step) % owners) for i in range(owners)]
        )

    def between(array, step):
        return lax.ppermute(array, "fsdp", [(i, (i + step) % groups) for i in range(groups)])

    mine = lax.dynamic_slice_in_dim(label_rows, core * share, share, 0)
    from_x = across(mine, 1)
    from_y = across(mine, 2)
    from_diagonal = jnp.concatenate(
        [across(from_x[:, :half], 2), across(from_y[:, half:], 1)], axis=1
    )

    hidden_rows = final_hidden[0].astype(jnp.float32)
    query_count = hidden_rows.shape[0]
    inverse_rms = lax.rsqrt(
        jnp.mean(hidden_rows * hidden_rows, axis=1, keepdims=True) + norm_epsilon
    )
    normed = hidden_rows * inverse_rms
    embedded = (normed * norm_gain).astype(jnp.bfloat16)
    owner_rows = jnp.repeat(active_blocks[0], QBLOCK, axis=0)
    codes = positives[0]
    code_block = codes // block_labels
    code_owner = jnp.sum(
        jnp.where(
            code_block[:, :, None] == jnp.arange(ACTIVE, dtype=jnp.int32),
            owner_rows[:, None, :],
            0,
        ),
        axis=2,
    )
    marks = jnp.concatenate([owner_rows, code_owner, codes % block_labels], axis=1)
    marks = jnp.pad(marks, ((0, 0), (0, META - marks.shape[1]))).astype(jnp.bfloat16)
    packet = jnp.concatenate([embedded, marks], axis=1)
    packets = jnp.concatenate(
        [packet] + [along(packet, step) for step in range(1, depth)], axis=0
    )

    fetched = jnp.stack([from_x, from_y, from_diagonal])
    pieces = [fetched] + [between(fetched, step) for step in range(1, groups)]
    plane_rows = jnp.concatenate(
        [label_rows] + [piece[k] for k in range(PLANE - 1) for piece in pieces], axis=0
    )
    within = jnp.arange(share, dtype=jnp.int32)
    fetched_labels = jnp.concatenate(
        [((core - step) % groups) * share + within for step in range(groups)]
    )
    column_label = jnp.concatenate(
        [jnp.arange(block_labels, dtype=jnp.int32)] + [fetched_labels] * (PLANE - 1)
    )
    column_owner = jnp.repeat(here ^ jnp.arange(PLANE, dtype=jnp.int32), block_labels)

    query_embed = packets[:, :width]
    query_marks = packets[:, width : width + 3 * ACTIVE].astype(jnp.int32)
    scores = lax.dot_general(
        query_embed, plane_rows, (((1,), (1,)), ((), ())), preferred_element_type=jnp.float32
    )
    active = jnp.zeros(scores.shape, jnp.bool_)
    positive = jnp.zeros(scores.shape, jnp.bool_)
    for k in range(ACTIVE):
        active |= query_marks[:, k : k + 1] == column_owner
        positive |= (query_marks[:, ACTIVE + k : ACTIVE + k + 1] == column_owner) & (
            query_marks[:, 2 * ACTIVE + k : 2 * ACTIVE + k + 1] == column_label
        )
    target_sign = jnp.where(positive, 1.0, -1.0)
    margin = jnp.maximum(1.0 - target_sign * scores, 0.0)
    slope = jnp.where(active, -2.0 * target_sign * margin, 0.0).astype(jnp.bfloat16)
    partial_grad = jnp.dot(slope, plane_rows, preferred_element_type=jnp.float32).astype(
        jnp.bfloat16
    )
    partial_grad = partial_grad.reshape(depth, query_count, width)
    embed_grad = partial_grad[0].astype(jnp.float32)
    for step in range(1, depth):
        embed_grad += along(partial_grad[step], -step).astype(jnp.float32)

    scaled = norm_gain * embed_grad
    resid = inverse_rms * (scaled - normed * jnp.mean(normed * scaled, axis=1, keepdims=True))
    resid_bf = resid.astype(jnp.bfloat16)

    line = jnp.stack([resid_bf] + [along(resid_bf, step) for step in range(1, depth)])
    line_x = across(line, 1)
    line_y = across(line, 2)
    line_diagonal = jnp.concatenate(
        [across(line_x[..., :half], 2), across(line_y[..., half:], 1)], axis=2
    )
    gathered = jnp.stack([line, line_x, line_y, line_diagonal])
    spots = jnp.arange(owners, dtype=jnp.int32)
    place = ((spots ^ here) % PLANE) * depth + (here // PLANE - spots // PLANE) % depth
    row_grads = jnp.take(
        gathered.reshape(owners, query_count, width), place, axis=0
    ).reshape(owners * query_count, width)

    gate_full = gate_pre.astype(jnp.float32)
    up_full = up_pre.astype(jnp.float32)
    sigma = jax.nn.sigmoid(gate_full)
    group_rows = gate_pre.shape[0] * gate_pre.shape[1]
    ff_local = gate_pre.shape[2]
    hidden_act = (gate_full * sigma * up_full).astype(jnp.bfloat16).reshape(group_rows, ff_local)

    slab = width // groups

    def slab_of(index):
        return lax.dynamic_slice_in_dim(row_grads, (index % groups) * slab, slab, 1)

    hidden_grad = jnp.dot(slab_of(core), down_weight, preferred_element_type=jnp.float32)
    down_grad = lax.dot_general(
        slab_of(core), hidden_act, (((0,), (0,)), ((), ())), preferred_element_type=jnp.float32
    )
    for step in range(1, groups):
        hidden_grad += jnp.dot(
            slab_of(core - step), between(down_weight, step), preferred_element_type=jnp.float32
        )
        down_grad += lax.dot_general(
            between(slab_of(core + step), step),
            between(hidden_act, step),
            (((0,), (0,)), ((), ())),
            preferred_element_type=jnp.float32,
        )
    hidden_grad = hidden_grad.reshape(gate_pre.shape)
    up_grad = (hidden_grad * gate_full * sigma).astype(jnp.bfloat16)
    gate_grad = (hidden_grad * up_full * sigma * (1.0 + gate_full * (1.0 - sigma))).astype(
        jnp.bfloat16
    )
    return (resid_bf[None], down_grad, gate_grad, up_grad)


def solution(mesh):
    placed = (
        P("label", "fsdp", None),
        P(),
        P("label", None, None),
        P("label", "fsdp", None),
        P("label", "fsdp", None),
        P(None, "fsdp", "label"),
        P(None, "fsdp", "label"),
        P("fsdp", "label"),
    )
    return jax.shard_map(
        shards,
        mesh=mesh,
        in_specs=placed,
        out_specs=(
            P("label", "fsdp", None),
            P("fsdp", "label"),
            P(None, "fsdp", "label"),
            P(None, "fsdp", "label"),
        ),
        check_vma=False,
    )
```

```python
import functools

import jax
import jax.numpy as jnp
from jax import lax
from jax.experimental import pallas as pl
from jax.experimental.pallas import tpu as pltpu
from jax.sharding import PartitionSpec as P

ACTIVE = 8
LBLOCK = 128
QBLOCK = 2
PLANE = 4
LANES = 128
FF_BLOCK = 256
COLUMNS = 512

norm_epsilon = 1e-06


def packet_kernel(hidden, gain, blocks, codes, packet):
    width = hidden.shape[1]
    rows = hidden[...].astype(jnp.float32)
    scale = lax.rsqrt(jnp.mean(rows * rows, axis=1, keepdims=True) + norm_epsilon)
    packet[:, :width] = (rows * scale * gain[...]).astype(jnp.bfloat16)

    def ones(shape, hit):
        at = [lax.broadcasted_iota(jnp.int32, shape, d) for d in range(2)]
        return hit(*at).astype(jnp.bfloat16)

    def times(left, right):
        return jnp.dot(left, right, preferred_element_type=jnp.float32)

    block_of = ones((rows.shape[0], blocks.shape[0]), lambda r, c: r // QBLOCK == c)
    owners = times(block_of, blocks[...].astype(jnp.bfloat16)).astype(jnp.bfloat16)
    found = codes[...]
    high = (found // LBLOCK).astype(jnp.bfloat16)
    low = (found % LBLOCK).astype(jnp.bfloat16)
    marks = sum(
        times(values, ones((values.shape[1], LANES), lambda r, c, n=n: c == r + n * ACTIVE))
        for n, values in enumerate((owners, high, low))
    )
    packet[:, width:] = marks.astype(jnp.bfloat16)


def slopes(embed, marks, rows, owner, first_label):
    scores = lax.dot_general(
        embed, rows, (((1,), (1,)), ((), ())), preferred_element_type=jnp.float32
    )
    slot = sum(
        jnp.where(marks[:, k : k + 1] == owner, k + 1, 0) for k in range(ACTIVE)
    )
    codes = marks[:, ACTIVE : 2 * ACTIVE] * LBLOCK + marks[:, 2 * ACTIVE : 3 * ACTIVE]
    label = lax.broadcasted_iota(jnp.int32, scores.shape, 1) + first_label
    code = (slot - 1) * LBLOCK + label
    positive = codes[:, 0:1] == code
    for k in range(1, ACTIVE):
        positive |= codes[:, k : k + 1] == code
    target_sign = jnp.where(positive, 1.0, -1.0)
    margin = jnp.maximum(1.0 - target_sign * scores, 0.0)
    return jnp.where(slot > 0, -2.0 * target_sign * margin, 0.0).astype(jnp.bfloat16)


def unpack(packets, width):
    embed = jnp.concatenate([packet[:, :width] for packet in packets], axis=0)
    marks = jnp.concatenate([packet[:, width:] for packet in packets], axis=0)
    return embed, marks.astype(jnp.int32)


def near_kernel(place, own, near, across, *refs):
    packets, (total, embed_out, marks_out) = refs[:-3], refs[-3:]
    width = own.shape[1]
    embed, marks = unpack(packets, width)
    embed_out[...] = embed
    marks_out[...] = marks
    here, parity = place[0], place[1]
    fetched = ((own, here), (near, here ^ (1 + parity)), (across, here ^ (2 - parity)))
    found = [(slopes(embed, marks, rows[...], owner, 0), rows) for rows, owner in fetched]
    for start in range(0, width, COLUMNS):
        span = slice(start, min(start + COLUMNS, width))
        total[:, span] = sum(
            jnp.dot(slope, rows[:, span], preferred_element_type=jnp.float32)
            for slope, rows in found
        )


def far_kernel(place, far, across, total, embed, marks, parts):
    width = far.shape[1]
    share = far.shape[0]
    embed, marks = embed[...], marks[...]
    here, parity = place[0], place[1]
    found = [
        slopes(embed, marks, far[...], here ^ 3, parity * share),
        slopes(embed, marks, across[...], here ^ 3, (1 - parity) * share),
    ]
    for start in range(0, width, COLUMNS):
        span = slice(start, min(start + COLUMNS, width))
        added = total[:, span] + sum(
            jnp.dot(slope, rows[:, span], preferred_element_type=jnp.float32)
            for slope, rows in zip(found, (far, across))
        )
        parts[:, :, span] = added.astype(jnp.bfloat16).reshape(
            parts.shape[0], parts.shape[1], added.shape[1]
        )


def pieces(extent):
    return [(start, min(start + FF_BLOCK, extent)) for start in range(0, extent, FF_BLOCK)]


def part_of(ref, rows, begin, columns):
    if columns == ref.shape[1]:
        return ref.at[slice(*rows)]
    return ref.at[slice(*rows), begin : begin + columns]


def hidden_kernel(groups, begin, first, last, *refs):
    refs = list(refs)
    order = refs.pop(0) if last else None
    share = None if first else refs.pop(0)
    grads = refs.pop(0)
    weights, refs = refs[:groups], refs[groups:]
    if last:
        gate, up, gate_grad, up_grad = refs
    else:
        (out,) = refs
    columns = grads.shape[2]
    for start, stop in pieces(weights[0].shape[0]):
        hidden_grad = sum(
            lax.dot_general(
                grads[n],
                weights[n][start:stop, begin : begin + columns],
                (((1,), (1,)), ((), ())),
                preferred_element_type=jnp.float32,
            )
            for n in range(groups)
        )
        if not first:
            hidden_grad = hidden_grad + share[:, start:stop]
        if not last:
            out[:, start:stop] = hidden_grad
            continue
        rows = gate.shape[1]
        for i in range(gate.shape[0]):
            block = order[i]
            part = hidden_grad[i * rows : (i + 1) * rows]
            gate_full = gate[block, :, start:stop].astype(jnp.float32)
            up_full = up[block, :, start:stop].astype(jnp.float32)
            sigma = jax.nn.sigmoid(gate_full)
            up_grad[block, :, start:stop] = (part * gate_full * sigma).astype(jnp.bfloat16)
            gate_grad[block, :, start:stop] = (
                part * up_full * sigma * (1.0 + gate_full * (1.0 - sigma))
            ).astype(jnp.bfloat16)


def down_kernel(groups, begin, kept, *refs):
    acts, slabs, refs = refs[:groups], refs[groups : 2 * groups], refs[2 * groups :]
    held, sems = refs[-2:]
    columns = slabs[0].shape[1]
    copies = []
    if kept:
        down_grad = refs[kept]
        for n in range(kept):
            copies.append(
                pltpu.make_async_copy(refs[n], refs[kept + 1 + n], sems.at[sems.shape[0] - 1 - n])
            )
            copies[-1].start()
    else:
        down_grad = refs[-3]
    for i, (start, stop) in enumerate(pieces(held.shape[0])):
        held[start:stop] = sum(
            jnp.dot(act[start:stop], slab[...], preferred_element_type=jnp.float32)
            for act, slab in zip(acts, slabs)
        )
        copies.append(
            pltpu.make_async_copy(
                held.at[start:stop],
                part_of(down_grad, (start, stop), begin, columns),
                sems.at[i],
            )
        )
        copies[-1].start()
    for copy in copies:
        copy.wait()


def params(megabytes):
    return pltpu.CompilerParams(vmem_limit_bytes=megabytes * 2**20)


def shards(
    final_hidden, norm_gain, label_weights, active_blocks, positives, gate_pre, up_pre, down_weight
):
    owners = lax.axis_size("label")
    groups = lax.axis_size("fsdp")
    depth = owners // PLANE
    here = lax.axis_index("label")
    core = lax.axis_index("fsdp")
    parity = core % 2
    label_rows = label_weights[0]
    block_labels, width = label_rows.shape
    share = block_labels // 2
    smem = pl.BlockSpec(memory_space=pltpu.SMEM)
    vmem = pl.BlockSpec(memory_space=pltpu.VMEM)
    anywhere = pl.BlockSpec(memory_space=pl.ANY)

    def swap(array, even, odd):
        pairs = [
            (i * groups + f, (i ^ (odd if f % 2 else even)) * groups + f)
            for i in range(owners)
            for f in range(groups)
        ]
        return lax.ppermute(array, ("label", "fsdp"), pairs)

    def mate(array):
        return lax.ppermute(array, "fsdp", [(f, f ^ 1) for f in range(groups)])

    def between(array, step):
        return lax.ppermute(array, "fsdp", [(i, (i + step) % groups) for i in range(groups)])

    near = swap(label_rows, 1, 2)
    near_mate = mate(near)
    far = swap(jnp.where(parity == 0, near[:share], near[share:]), 2, 1)

    query_count = final_hidden.shape[1]
    packet = pl.pallas_call(
        packet_kernel,
        out_shape=jax.ShapeDtypeStruct((query_count, width + LANES), jnp.bfloat16),
        in_specs=[vmem] * 4,
        out_specs=vmem,
        compiler_params=params(16),
    )(final_hidden[0], norm_gain[None], active_blocks[0], positives[0])
    packets = [packet] + [swap(packet, PLANE * s, PLANE * s) for s in range(1, depth)]

    plane_masks = jnp.stack([0 * parity, 1 + parity, 2 - parity, 0 * parity + 3])
    order = here ^ (
        plane_masks[:, None] + PLANE * jnp.arange(depth, dtype=jnp.int32)[None, :]
    ).reshape(owners)
    order = order.astype(jnp.int32)
    gate_full = gate_pre.astype(jnp.float32)
    sigma = jax.nn.sigmoid(gate_full)
    hidden_act = (gate_full * sigma * up_pre.astype(jnp.float32)).astype(jnp.bfloat16)
    group_rows = owners * query_count
    ff_local = gate_pre.shape[2]
    act = jnp.take(hidden_act, order, axis=0).reshape(group_rows, ff_local).T
    weights = [down_weight.T] + [between(down_weight, n).T for n in range(1, groups)]

    place = jnp.stack([here, parity]).astype(jnp.int32)
    line_rows = depth * query_count
    total, embed, marks = pl.pallas_call(
        near_kernel,
        out_shape=[
            jax.ShapeDtypeStruct((line_rows, width), jnp.float32),
            jax.ShapeDtypeStruct((line_rows, width), jnp.bfloat16),
            jax.ShapeDtypeStruct((line_rows, LANES), jnp.int32),
        ],
        in_specs=[smem] + [vmem] * (3 + depth),
        out_specs=[vmem] * 3,
        compiler_params=params(24),
        cost_estimate=pl.CostEstimate(
            flops=12 * line_rows * block_labels * width,
            bytes_accessed=6 * block_labels * width,
            transcendentals=0,
        ),
    )(place, label_rows, near, near_mate, *packets)
    far_mate = mate(far)
    parts = pl.pallas_call(
        far_kernel,
        out_shape=jax.ShapeDtypeStruct((depth, query_count, width), jnp.bfloat16),
        in_specs=[smem] + [vmem] * 5,
        out_specs=vmem,
        compiler_params=params(24),
    )(place, far, far_mate, total, embed, marks)
    embed_grad = parts[0].astype(jnp.float32)
    for s in range(1, depth):
        embed_grad += swap(parts[s], PLANE * s, PLANE * s).astype(jnp.float32)

    embed_grad, act = lax.optimization_barrier((embed_grad, act))
    acts = [act] + [between(act, n) for n in range(1, groups)]
    hidden_rows = final_hidden[0].astype(jnp.float32)
    inverse_rms = lax.rsqrt(
        jnp.mean(hidden_rows * hidden_rows, axis=1, keepdims=True) + norm_epsilon
    )
    normed = hidden_rows * inverse_rms
    scaled = norm_gain * embed_grad
    resid = inverse_rms * (scaled - normed * jnp.mean(normed * scaled, axis=1, keepdims=True))
    resid_bf = resid.astype(jnp.bfloat16)

    slab = width // groups
    cuts = [0, slab // 2, slab] if slab % (2 * LANES) == 0 else [0, slab]
    own = jnp.stack(
        [
            lax.dynamic_slice_in_dim(resid_bf, ((core - n) % groups) * slab, slab, 1)
            for n in range(groups)
        ]
    )
    lines = [
        [own[..., begin:end]]
        + [swap(own[..., begin:end], PLANE * s, PLANE * s) for s in range(1, depth)]
        for begin, end in zip(cuts, cuts[1:])
    ]

    def hidden(part, begin, share, final, weights):
        columns = part.shape[2]
        shapes = [jax.ShapeDtypeStruct((group_rows, ff_local), jnp.float32)]
        operands, smems = [part, *weights], 0
        if share is not None:
            operands = [share] + operands
        if final:
            shapes = [jax.ShapeDtypeStruct(gate_pre.shape, jnp.bfloat16)] * 2
            operands, smems = [order] + operands + [gate_pre, up_pre], 1
        return pl.pallas_call(
            functools.partial(hidden_kernel, groups, begin, share is None, final),
            out_shape=shapes,
            in_specs=[smem] * smems + [vmem] * (len(operands) - smems),
            out_specs=[vmem] * len(shapes),
            compiler_params=params(16),
            cost_estimate=matmul_cost(columns, 2 * ff_local * columns * groups),
        )(*operands)

    def matmul_cost(columns, more):
        return pl.CostEstimate(
            flops=2 * groups * group_rows * columns * ff_local,
            bytes_accessed=more,
            transcendentals=0,
        )

    def down(part, begin, so_far, kept):
        columns = part.shape[2]
        slabs = [part[0]] + [between(part[groups - n], n) for n in range(1, groups)]
        outs = pl.pallas_call(
            functools.partial(down_kernel, groups, begin, len(kept)),
            out_shape=[jax.ShapeDtypeStruct((ff_local, slab), jnp.float32)]
            + [jax.ShapeDtypeStruct(array.shape, array.dtype) for array in kept],
            in_specs=[vmem] * (2 * groups) + [anywhere] * (len(so_far) + len(kept)),
            out_specs=[anywhere] + [vmem] * len(kept),
            scratch_shapes=[
                pltpu.VMEM((ff_local, columns), jnp.float32),
                pltpu.SemaphoreType.DMA((len(pieces(ff_local)) + len(kept),)),
            ],
            input_output_aliases={2 * groups: 0} if so_far else {},
            compiler_params=params(24),
            cost_estimate=matmul_cost(columns, 4 * ff_local * columns),
        )(*acts, *slabs, *so_far, *kept)
        return list(outs[:1]), list(outs[1:])

    def begin_plane(line):
        line = jnp.concatenate(line, axis=1)
        return line, swap(line, 1, 2), swap(line, 2, 1)

    share, so_far = None, []
    line, first, second = begin_plane(lines[0])
    for k, (begin, end) in enumerate(zip(cuts, cuts[1:])):
        final = k == len(lines) - 1
        if not final:
            first, lines[k + 1] = lax.optimization_barrier((first, lines[k + 1]))
        third = swap(first, 2, 1)
        if not final:
            ahead = begin_plane(lines[k + 1])
            third, ahead = lax.optimization_barrier((third, ahead))
        elif so_far:
            third, share, so_far = lax.optimization_barrier((third, share, so_far))
        part = jnp.concatenate([line, first, second, third], axis=1)
        if final:
            gate_grad, up_grad = hidden(part, begin, share, final, weights)
            so_far, _ = down(part, begin, so_far, [])
        else:
            so_far, kept = down(part, begin, so_far, weights[1:])
            weights = weights[:1] + kept
            (share,) = hidden(part, begin, share, final, weights)
            line, first, second = ahead
    return (resid_bf[None], so_far[0].T, gate_grad, up_grad)


def solution(mesh):
    placed = (
        P("label", "fsdp", None),
        P(),
        P("label", None, None),
        P("label", "fsdp", None),
        P("label", "fsdp", None),
        P(None, "fsdp", "label"),
        P(None, "fsdp", "label"),
        P("fsdp", "label"),
    )
    return jax.shard_map(
        shards,
        mesh=mesh,
        in_specs=placed,
        out_specs=(
            P("label", "fsdp", None),
            P("fsdp", "label"),
            P(None, "fsdp", "label"),
            P(None, "fsdp", "label"),
        ),
        check_vma=False,
    )
```

```python
import functools

import jax
import jax.numpy as jnp
from jax import lax
from jax.experimental import pallas as pl
from jax.experimental.pallas import tpu as pltpu
from jax.sharding import PartitionSpec as P

ACTIVE = 8
LBLOCK = 128
QBLOCK = 2
PLANE = 4
LANES = 128
FF_BLOCK = 256
COLUMNS = 512

norm_epsilon = 1e-06


def packet_kernel(hidden, gain, blocks, codes, packet):
    width = hidden.shape[1]
    rows = hidden[...].astype(jnp.float32)
    scale = lax.rsqrt(jnp.mean(rows * rows, axis=1, keepdims=True) + norm_epsilon)
    packet[:, :width] = (rows * scale * gain[...]).astype(jnp.bfloat16)

    def ones(shape, hit):
        at = [lax.broadcasted_iota(jnp.int32, shape, d) for d in range(2)]
        return hit(*at).astype(jnp.bfloat16)

    def times(left, right):
        return jnp.dot(left, right, preferred_element_type=jnp.float32)

    block_of = ones((rows.shape[0], blocks.shape[0]), lambda r, c: r // QBLOCK == c)
    owners = times(block_of, blocks[...].astype(jnp.bfloat16)).astype(jnp.bfloat16)
    found = codes[...]
    high = (found // LBLOCK).astype(jnp.bfloat16)
    low = (found % LBLOCK).astype(jnp.bfloat16)
    marks = sum(
        times(values, ones((values.shape[1], LANES), lambda r, c, n=n: c == r + n * ACTIVE))
        for n, values in enumerate((owners, high, low))
    )
    packet[:, width:] = marks.astype(jnp.bfloat16)


def slopes(embed, marks, rows, owner, first_label):
    scores = lax.dot_general(
        embed, rows, (((1,), (1,)), ((), ())), preferred_element_type=jnp.float32
    )
    slot = sum(
        jnp.where(marks[:, k : k + 1] == owner, k + 1, 0) for k in range(ACTIVE)
    )
    codes = marks[:, ACTIVE : 2 * ACTIVE] * LBLOCK + marks[:, 2 * ACTIVE : 3 * ACTIVE]
    label = lax.broadcasted_iota(jnp.int32, scores.shape, 1) + first_label
    code = (slot - 1) * LBLOCK + label
    positive = codes[:, 0:1] == code
    for k in range(1, ACTIVE):
        positive |= codes[:, k : k + 1] == code
    target_sign = jnp.where(positive, 1.0, -1.0)
    margin = jnp.maximum(1.0 - target_sign * scores, 0.0)
    return jnp.where(slot > 0, -2.0 * target_sign * margin, 0.0).astype(jnp.bfloat16)


def unpack(packets, width):
    embed = jnp.concatenate([packet[:, :width] for packet in packets], axis=0)
    marks = jnp.concatenate([packet[:, width:] for packet in packets], axis=0)
    return embed, marks.astype(jnp.int32)


def near_kernel(place, own, near, across, *refs):
    packets, (total, embed_out, marks_out) = refs[:-3], refs[-3:]
    width = own.shape[1]
    embed, marks = unpack(packets, width)
    embed_out[...] = embed
    marks_out[...] = marks
    here, parity = place[0], place[1]
    fetched = ((own, here), (near, here ^ (1 + parity)), (across, here ^ (2 - parity)))
    found = [(slopes(embed, marks, rows[...], owner, 0), rows) for rows, owner in fetched]
    for start in range(0, width, COLUMNS):
        span = slice(start, min(start + COLUMNS, width))
        total[:, span] = sum(
            jnp.dot(slope, rows[:, span], preferred_element_type=jnp.float32)
            for slope, rows in found
        )


def far_kernel(depth, place, far, across, total, embed, marks, *refs):
    parts = refs[-depth:]
    width = far.shape[1]
    share = far.shape[0]
    embed, marks = embed[...], marks[...]
    here, parity = place[0], place[1]
    found = [
        slopes(embed, marks, far[...], here ^ 3, parity * share),
        slopes(embed, marks, across[...], here ^ 3, (1 - parity) * share),
    ]
    for start in range(0, width, COLUMNS):
        span = slice(start, min(start + COLUMNS, width))
        added = total[:, span] + sum(
            jnp.dot(slope, rows[:, span], preferred_element_type=jnp.float32)
            for slope, rows in zip(found, (far, across))
        )
        rows = parts[0].shape[0]
        for s, part in enumerate(parts):
            part[:, span] = added[s * rows : (s + 1) * rows].astype(jnp.bfloat16)


def resid_kernel(hidden, gain, ready, *refs):
    parts, out = refs[:-1], refs[-1]
    rows = hidden[...].astype(jnp.float32)
    scale = lax.rsqrt(jnp.mean(rows * rows, axis=1, keepdims=True) + norm_epsilon)
    normed = rows * scale
    scaled = gain[...] * sum(part[...].astype(jnp.float32) for part in parts)
    out[...] = (
        scale * (scaled - normed * jnp.mean(normed * scaled, axis=1, keepdims=True))
    ).astype(jnp.bfloat16)


def pieces(extent):
    return [(start, min(start + FF_BLOCK, extent)) for start in range(0, extent, FF_BLOCK)]


def hold_kernel(*refs):
    sems, half = refs[-1], len(refs) // 2
    copies = [
        pltpu.make_async_copy(refs[n], refs[half + n], sems.at[n]) for n in range(half)
    ]
    for copy in copies:
        copy.start()
    for copy in copies:
        copy.wait()


def act_kernel(order, gate, up, act, rows_held):
    rows = gate.shape[1]
    for i in range(gate.shape[0]):
        gate_full = gate[order[i]].astype(jnp.float32)
        up_full = up[order[i]].astype(jnp.float32)
        rows_held[i * rows : (i + 1) * rows] = gate_full * jax.nn.sigmoid(gate_full) * up_full
    for start, stop in pieces(rows_held.shape[1]):
        act[start:stop] = rows_held[:, start:stop].T.astype(jnp.bfloat16)


def hidden_kernel(groups, grads, *refs):
    weights, hidden_grad = refs[:groups], refs[groups]
    for start, stop in pieces(hidden_grad.shape[1]):
        hidden_grad[:, start:stop] = sum(
            lax.dot_general(
                grads[n],
                weights[n][start:stop],
                (((1,), (1,)), ((), ())),
                preferred_element_type=jnp.float32,
            )
            for n in range(groups)
        )


def last_kernel(groups, order, hidden_grad, gate, up, *refs):
    acts, slabs, refs = refs[:groups], refs[groups : 2 * groups], refs[2 * groups :]
    down_grad, gate_grad, up_grad, gate_held, up_held, held, sems = refs
    spans = pieces(held.shape[0])
    rows, blocks = gate.shape[1], gate.shape[0]
    copies = []
    for n, (start, stop) in enumerate(spans):
        held[start:stop] = sum(
            jnp.dot(act[start:stop], slab[...], preferred_element_type=jnp.float32)
            for act, slab in zip(acts, slabs)
        )
        copies.append(
            pltpu.make_async_copy(held.at[start:stop], down_grad.at[start:stop], sems.at[n])
        )
        copies[-1].start()
        turns = max(1, len(spans) - 1)
        for i in range(n * blocks // turns, min(blocks, (n + 1) * blocks // turns)):
            block = order[i]
            part = hidden_grad[i * rows : (i + 1) * rows]
            gate_full = gate[block].astype(jnp.float32)
            up_full = up[block].astype(jnp.float32)
            sigma = jax.nn.sigmoid(gate_full)
            up_held[block] = (part * gate_full * sigma).astype(jnp.bfloat16)
            gate_held[block] = (
                part * up_full * sigma * (1.0 + gate_full * (1.0 - sigma))
            ).astype(jnp.bfloat16)
        if n == turns - 1:
            copies.append(pltpu.make_async_copy(gate_held, gate_grad, sems.at[len(spans)]))
            copies.append(pltpu.make_async_copy(up_held, up_grad, sems.at[len(spans) + 1]))
            copies[-2].start()
            copies[-1].start()
    for copy in copies:
        copy.wait()


def params(megabytes):
    return pltpu.CompilerParams(vmem_limit_bytes=megabytes * 2**20)


def shards(
    final_hidden, norm_gain, label_weights, active_blocks, positives, gate_pre, up_pre, down_weight
):
    owners = lax.axis_size("label")
    groups = lax.axis_size("fsdp")
    depth = owners // PLANE
    here = lax.axis_index("label")
    core = lax.axis_index("fsdp")
    parity = core % 2
    label_rows = label_weights[0]
    block_labels, width = label_rows.shape
    share = block_labels // 2
    smem = pl.BlockSpec(memory_space=pltpu.SMEM)
    vmem = pl.BlockSpec(memory_space=pltpu.VMEM)
    anywhere = pl.BlockSpec(memory_space=pl.ANY)

    def swap(array, even, odd):
        pairs = [
            (i * groups + f, (i ^ (odd if f % 2 else even)) * groups + f)
            for i in range(owners)
            for f in range(groups)
        ]
        return lax.ppermute(array, ("label", "fsdp"), pairs)

    def mate(array):
        return lax.ppermute(array, "fsdp", [(f, f ^ 1) for f in range(groups)])

    def between(array, step):
        return lax.ppermute(array, "fsdp", [(i, (i + step) % groups) for i in range(groups)])

    query_count = final_hidden.shape[1]
    packet = pl.pallas_call(
        packet_kernel,
        out_shape=jax.ShapeDtypeStruct((query_count, width + LANES), jnp.bfloat16),
        in_specs=[vmem] * 4,
        out_specs=vmem,
        compiler_params=params(16),
    )(final_hidden[0], norm_gain[None], active_blocks[0], positives[0])

    def along(piece):
        line = [piece]
        for s in range(1, depth):
            step = s & -s
            line.append(swap(line[s - step], PLANE * step, PLANE * step))
        return line

    packets = along(packet)

    near = swap(label_rows, 1, 2)
    near_mate = mate(near)
    passing = jnp.where(parity == 0, near[:share], near[share:])
    passing, ready = lax.optimization_barrier((passing, [packets[depth // 2][:8, :LANES]]))
    far = swap(passing, 2, 1)
    place = jnp.stack([here, parity]).astype(jnp.int32)

    plane_masks = jnp.stack([0 * parity, 1 + parity, 2 - parity, 0 * parity + 3])
    order = here ^ (
        PLANE * jnp.arange(depth, dtype=jnp.int32)[:, None] + plane_masks[None, :]
    ).reshape(owners)
    order = order.astype(jnp.int32)
    group_rows = owners * query_count
    ff_local = gate_pre.shape[2]
    weights = [down_weight.T] + [between(down_weight, n).T for n in range(1, groups)]
    others = pl.pallas_call(
        hold_kernel,
        out_shape=[jax.ShapeDtypeStruct(other.shape, other.dtype) for other in weights[1:]],
        in_specs=[anywhere] * (groups - 1),
        out_specs=[vmem] * (groups - 1),
        scratch_shapes=[pltpu.SemaphoreType.DMA((groups,))],
        compiler_params=params(16),
        cost_estimate=pl.CostEstimate(
            flops=0, bytes_accessed=4 * ff_local * width, transcendentals=0
        ),
    )(*weights[1:])
    weights = weights[:1] + list(others)
    act = pl.pallas_call(
        act_kernel,
        out_shape=jax.ShapeDtypeStruct((ff_local, group_rows), jnp.bfloat16),
        in_specs=[smem, vmem, vmem],
        out_specs=vmem,
        scratch_shapes=[pltpu.VMEM((group_rows, ff_local), jnp.float32)],
        compiler_params=params(16),
        cost_estimate=pl.CostEstimate(
            flops=8 * group_rows * ff_local,
            bytes_accessed=8 * group_rows * ff_local,
            transcendentals=group_rows * ff_local,
        ),
    )(order, gate_pre, up_pre)
    acts = [act] + [between(act, n) for n in range(1, groups)]

    far, more = lax.optimization_barrier(
        (far, [array[:8, :LANES] for array in [act, *packets[1:]]])
    )
    far_mate = mate(far)
    ready = ready + more
    line_rows = depth * query_count
    total, embed, marks = pl.pallas_call(
        near_kernel,
        out_shape=[
            jax.ShapeDtypeStruct((line_rows, width), jnp.float32),
            jax.ShapeDtypeStruct((line_rows, width), jnp.bfloat16),
            jax.ShapeDtypeStruct((line_rows, LANES), jnp.int32),
        ],
        in_specs=[smem] + [vmem] * (3 + depth),
        out_specs=[vmem] * 3,
        compiler_params=params(16),
        cost_estimate=pl.CostEstimate(
            flops=12 * line_rows * block_labels * width,
            bytes_accessed=6 * block_labels * width,
            transcendentals=0,
        ),
    )(place, label_rows, near, near_mate, *packets)
    parts = pl.pallas_call(
        functools.partial(far_kernel, depth),
        out_shape=[jax.ShapeDtypeStruct((query_count, width), jnp.bfloat16)] * depth,
        in_specs=[smem] + [vmem] * 5 + [anywhere] * len(ready),
        out_specs=[vmem] * depth,
        compiler_params=params(16),
    )(place, far, far_mate, total, embed, marks, *ready)
    resid_bf = pl.pallas_call(
        resid_kernel,
        out_shape=jax.ShapeDtypeStruct((query_count, width), jnp.bfloat16),
        in_specs=[vmem, vmem, anywhere] + [vmem] * depth,
        out_specs=vmem,
        compiler_params=params(16),
    )(
        final_hidden[0],
        norm_gain[None],
        weights[-1],
        parts[0],
        *[swap(parts[s], PLANE * s, PLANE * s) for s in range(1, depth)],
    )

    slab = width // groups
    own = jnp.stack(
        [
            lax.dynamic_slice_in_dim(resid_bf, ((core - n) % groups) * slab, slab, 1)
            for n in range(groups)
        ]
    )
    line = along(own)
    rows = []
    for some in [line[: depth // 2]] + [[piece] for piece in line[depth // 2 :]]:
        some = jnp.concatenate(some, axis=1)
        first, second = swap(some, 1, 2), swap(some, 2, 1)
        found = (some, first, second, swap(first, 2, 1))
        for start in range(0, some.shape[1], query_count):
            rows.append(
                jnp.concatenate([part[:, start : start + query_count] for part in found], axis=1)
            )
    early = jnp.concatenate(rows[: depth // 2], axis=1)
    late = jnp.concatenate(rows[depth // 2 :], axis=1)
    grads = jnp.concatenate([early, late], axis=1)
    slabs = [grads[0]] + [
        jnp.concatenate([between(half[groups - n], n) for half in (early, late)], axis=0)
        for n in range(1, groups)
    ]

    hidden_grad = pl.pallas_call(
        functools.partial(hidden_kernel, groups),
        out_shape=jax.ShapeDtypeStruct((group_rows, ff_local), jnp.float32),
        in_specs=[vmem] * (1 + groups),
        out_specs=vmem,
        compiler_params=params(16),
        cost_estimate=pl.CostEstimate(
            flops=2 * group_rows * width * ff_local,
            bytes_accessed=2 * ff_local * width,
            transcendentals=0,
        ),
    )(grads, *weights)
    down_grad, gate_grad, up_grad = pl.pallas_call(
        functools.partial(last_kernel, groups),
        out_shape=[jax.ShapeDtypeStruct((ff_local, slab), jnp.float32)]
        + [jax.ShapeDtypeStruct(gate_pre.shape, jnp.bfloat16)] * 2,
        in_specs=[smem] + [vmem] * (3 + 2 * groups),
        out_specs=[anywhere] * 3,
        scratch_shapes=[pltpu.VMEM(gate_pre.shape, jnp.bfloat16)] * 2
        + [
            pltpu.VMEM((ff_local, slab), jnp.float32),
            pltpu.SemaphoreType.DMA((len(pieces(ff_local)) + 2,)),
        ],
        compiler_params=params(20),
        cost_estimate=pl.CostEstimate(
            flops=2 * group_rows * width * ff_local,
            bytes_accessed=4 * ff_local * slab + 8 * group_rows * ff_local,
            transcendentals=group_rows * ff_local,
        ),
    )(order, hidden_grad, gate_pre, up_pre, *acts, *slabs)
    return (resid_bf[None], down_grad.T, gate_grad, up_grad)


def solution(mesh):
    placed = (
        P("label", "fsdp", None),
        P(),
        P("label", None, None),
        P("label", "fsdp", None),
        P("label", "fsdp", None),
        P(None, "fsdp", "label"),
        P(None, "fsdp", "label"),
        P("fsdp", "label"),
    )
    return jax.shard_map(
        shards,
        mesh=mesh,
        in_specs=placed,
        out_specs=(
            P("label", "fsdp", None),
            P("fsdp", "label"),
            P(None, "fsdp", "label"),
            P(None, "fsdp", "label"),
        ),
        check_vma=False,
    )
```

```python
import functools

import jax
import jax.numpy as jnp
from jax import lax
from jax.experimental import pallas as pl
from jax.experimental.pallas import tpu as pltpu
from jax.sharding import PartitionSpec as P

ACTIVE = 8
LBLOCK = 128
QBLOCK = 2
PLANE = 4
LANES = 128
FF_BLOCK = 256
COLUMNS = 512

norm_epsilon = 1e-06


def packet_kernel(hidden, gain, blocks, codes, packet):
    width = hidden.shape[1]
    rows = hidden[...].astype(jnp.float32)
    scale = lax.rsqrt(jnp.mean(rows * rows, axis=1, keepdims=True) + norm_epsilon)
    packet[:, :width] = (rows * scale * gain[...][None]).astype(jnp.bfloat16)

    def ones(shape, hit):
        at = [lax.broadcasted_iota(jnp.int32, shape, d) for d in range(2)]
        return hit(*at).astype(jnp.bfloat16)

    def times(left, right):
        return jnp.dot(left, right, preferred_element_type=jnp.float32)

    block_of = ones((rows.shape[0], blocks.shape[0]), lambda r, c: r // QBLOCK == c)
    owners = times(block_of, blocks[...].astype(jnp.bfloat16)).astype(jnp.bfloat16)
    found = codes[...]
    high = (found // LBLOCK).astype(jnp.bfloat16)
    low = (found % LBLOCK).astype(jnp.bfloat16)
    def spot(n):
        return ones((ACTIVE, LANES), lambda r, c: c == r + n * ACTIVE)

    marks = times(owners, spot(0)) + sum(
        lax.dot_general(
            values, spot(n + 1), (((0,), (0,)), ((), ())), preferred_element_type=jnp.float32
        )
        for n, values in enumerate((high, low))
    )
    packet[:, width:] = marks.astype(jnp.bfloat16)


def slopes(embed, marks, rows, owner, first_label):
    scores = lax.dot_general(
        embed, rows, (((1,), (1,)), ((), ())), preferred_element_type=jnp.float32
    )
    slot = sum(
        jnp.where(marks[:, k : k + 1] == owner, k + 1, 0) for k in range(ACTIVE)
    )
    codes = marks[:, ACTIVE : 2 * ACTIVE] * LBLOCK + marks[:, 2 * ACTIVE : 3 * ACTIVE]
    label = lax.broadcasted_iota(jnp.int32, scores.shape, 1) + first_label
    code = (slot - 1) * LBLOCK + label
    positive = codes[:, 0:1] == code
    for k in range(1, ACTIVE):
        positive |= codes[:, k : k + 1] == code
    target_sign = jnp.where(positive, 1.0, -1.0)
    margin = jnp.maximum(1.0 - target_sign * scores, 0.0)
    return jnp.where(slot > 0, -2.0 * target_sign * margin, 0.0).astype(jnp.bfloat16)


def unpack(packets, width):
    embed = jnp.concatenate([packet[:, :width] for packet in packets], axis=0)
    marks = jnp.concatenate([packet[:, width:] for packet in packets], axis=0)
    return embed, marks.astype(jnp.int32)


def near_kernel(place, own, near, across, *refs):
    packets, (total, embed_out, marks_out) = refs[:-3], refs[-3:]
    width = own.shape[1]
    embed, marks = unpack(packets, width)
    embed_out[...] = embed
    marks_out[...] = marks
    here, parity = place[0], place[1]
    fetched = ((own, here), (near, here ^ (1 + parity)), (across, here ^ (2 - parity)))
    found = [(slopes(embed, marks, rows[...], owner, 0), rows) for rows, owner in fetched]
    for start in range(0, width, COLUMNS):
        span = slice(start, min(start + COLUMNS, width))
        total[:, span] = sum(
            jnp.dot(slope, rows[:, span], preferred_element_type=jnp.float32)
            for slope, rows in found
        )


def far_kernel(depth, place, far, across, total, embed, marks, *refs):
    parts = refs[-depth:]
    width = far.shape[1]
    share = far.shape[0]
    embed, marks = embed[...], marks[...]
    here, parity = place[0], place[1]
    found = [
        slopes(embed, marks, far[...], here ^ 3, parity * share),
        slopes(embed, marks, across[...], here ^ 3, (1 - parity) * share),
    ]
    for start in range(0, width, COLUMNS):
        span = slice(start, min(start + COLUMNS, width))
        added = total[:, span] + sum(
            jnp.dot(slope, rows[:, span], preferred_element_type=jnp.float32)
            for slope, rows in zip(found, (far, across))
        )
        rows = parts[0].shape[0]
        for s, part in enumerate(parts):
            part[:, span] = added[s * rows : (s + 1) * rows].astype(jnp.bfloat16)


def resid_kernel(hidden, gain, ready, *refs):
    parts, out, again = refs[:-2], refs[-2], refs[-1]
    rows = hidden[...].astype(jnp.float32)
    scale = lax.rsqrt(jnp.mean(rows * rows, axis=1, keepdims=True) + norm_epsilon)
    normed = rows * scale
    scaled = gain[...][None] * sum(part[...].astype(jnp.float32) for part in parts)
    out[...] = (
        scale * (scaled - normed * jnp.mean(normed * scaled, axis=1, keepdims=True))
    ).astype(jnp.bfloat16)
    again[...] = out[...]


def pieces(extent):
    return [(start, min(start + FF_BLOCK, extent)) for start in range(0, extent, FF_BLOCK)]


def hold_kernel(*refs):
    sems, half = refs[-1], len(refs) // 2
    copies = [
        pltpu.make_async_copy(refs[n], refs[half + n], sems.at[n]) for n in range(half)
    ]
    for copy in copies:
        copy.start()
    for copy in copies:
        copy.wait()


def act_kernel(order, gate, up, act, rows_held):
    rows = gate.shape[1]
    for i in range(gate.shape[0]):
        gate_full = gate[order[i]].astype(jnp.float32)
        up_full = up[order[i]].astype(jnp.float32)
        rows_held[i * rows : (i + 1) * rows] = gate_full * jax.nn.sigmoid(gate_full) * up_full
    for start, stop in pieces(rows_held.shape[1]):
        act[start:stop] = rows_held[:, start:stop].T.astype(jnp.bfloat16)


def hidden_kernel(groups, grads, *refs):
    weights, hidden_grad = refs[:groups], refs[groups]
    for start, stop in pieces(hidden_grad.shape[1]):
        hidden_grad[:, start:stop] = sum(
            lax.dot_general(
                grads[n],
                weights[n][start:stop],
                (((1,), (1,)), ((), ())),
                preferred_element_type=jnp.float32,
            )
            for n in range(groups)
        )


def last_kernel(groups, order, hidden_grad, gate, up, *refs):
    acts, slabs, refs = refs[:groups], refs[groups : 2 * groups], refs[2 * groups :]
    down_grad, gate_grad, up_grad, gate_held, up_held, held, sems = refs
    spans = pieces(held.shape[0])
    rows, blocks = gate.shape[1], gate.shape[0]
    copies = []
    for n, (start, stop) in enumerate(spans):
        held[start:stop] = sum(
            jnp.dot(act[start:stop], slab[...], preferred_element_type=jnp.float32)
            for act, slab in zip(acts, slabs)
        )
        copies.append(
            pltpu.make_async_copy(held.at[start:stop], down_grad.at[start:stop], sems.at[n])
        )
        copies[-1].start()
        turns = max(1, len(spans) - 1)
        for i in range(n * blocks // turns, min(blocks, (n + 1) * blocks // turns)):
            block = order[i]
            part = hidden_grad[i * rows : (i + 1) * rows]
            gate_full = gate[block].astype(jnp.float32)
            up_full = up[block].astype(jnp.float32)
            sigma = jax.nn.sigmoid(gate_full)
            up_held[block] = (part * gate_full * sigma).astype(jnp.bfloat16)
            gate_held[block] = (
                part * up_full * sigma * (1.0 + gate_full * (1.0 - sigma))
            ).astype(jnp.bfloat16)
        if n == turns - 1:
            copies.append(pltpu.make_async_copy(gate_held, gate_grad, sems.at[len(spans)]))
            copies.append(pltpu.make_async_copy(up_held, up_grad, sems.at[len(spans) + 1]))
            copies[-2].start()
            copies[-1].start()
    for copy in copies:
        copy.wait()


def params(megabytes):
    return pltpu.CompilerParams(vmem_limit_bytes=megabytes * 2**20)


def shards(
    final_hidden, norm_gain, label_weights, active_blocks, positives, gate_pre, up_pre, down_weight
):
    owners = lax.axis_size("label")
    groups = lax.axis_size("fsdp")
    depth = owners // PLANE
    here = lax.axis_index("label")
    core = lax.axis_index("fsdp")
    parity = core % 2
    label_rows = label_weights[0]
    block_labels, width = label_rows.shape
    share = block_labels // 2
    smem = pl.BlockSpec(memory_space=pltpu.SMEM)
    vmem = pl.BlockSpec(memory_space=pltpu.VMEM)
    anywhere = pl.BlockSpec(memory_space=pl.ANY)

    def swap(array, even, odd):
        pairs = [
            (i * groups + f, (i ^ (odd if f % 2 else even)) * groups + f)
            for i in range(owners)
            for f in range(groups)
        ]
        return lax.ppermute(array, ("label", "fsdp"), pairs)

    def mate(array):
        return lax.ppermute(array, "fsdp", [(f, f ^ 1) for f in range(groups)])

    def between(array, step):
        return lax.ppermute(array, "fsdp", [(i, (i + step) % groups) for i in range(groups)])

    query_count = final_hidden.shape[1]
    packet = pl.pallas_call(
        packet_kernel,
        out_shape=jax.ShapeDtypeStruct((query_count, width + LANES), jnp.bfloat16),
        in_specs=[vmem] * 4,
        out_specs=vmem,
        compiler_params=params(16),
    )(final_hidden[0], norm_gain, active_blocks[0], positives[0].T)

    def along(piece):
        line = [piece]
        for s in range(1, depth):
            step = s & -s
            line.append(swap(line[s - step], PLANE * step, PLANE * step))
        return line

    packets = along(packet)

    near = swap(label_rows, 1, 2)
    near_mate = mate(near)
    passing = jnp.where(parity == 0, near[:share], near[share:])
    passing, ready = lax.optimization_barrier((passing, [packets[depth // 2][:8, :LANES]]))
    far = swap(passing, 2, 1)
    place = jnp.stack([here, parity]).astype(jnp.int32)

    plane_masks = jnp.stack([0 * parity, 1 + parity, 2 - parity, 0 * parity + 3])
    order = here ^ (
        PLANE * jnp.arange(depth, dtype=jnp.int32)[:, None] + plane_masks[None, :]
    ).reshape(owners)
    order = order.astype(jnp.int32)
    group_rows = owners * query_count
    ff_local = gate_pre.shape[2]
    weights = [down_weight.T] + [between(down_weight, n).T for n in range(1, groups)]
    others = pl.pallas_call(
        hold_kernel,
        out_shape=[jax.ShapeDtypeStruct(other.shape, other.dtype) for other in weights[1:]],
        in_specs=[anywhere] * (groups - 1),
        out_specs=[vmem] * (groups - 1),
        scratch_shapes=[pltpu.SemaphoreType.DMA((groups,))],
        compiler_params=params(16),
        cost_estimate=pl.CostEstimate(
            flops=0, bytes_accessed=4 * ff_local * width, transcendentals=0
        ),
    )(*weights[1:])
    weights = weights[:1] + list(others)
    act = pl.pallas_call(
        act_kernel,
        out_shape=jax.ShapeDtypeStruct((ff_local, group_rows), jnp.bfloat16),
        in_specs=[smem, vmem, vmem],
        out_specs=vmem,
        scratch_shapes=[pltpu.VMEM((group_rows, ff_local), jnp.float32)],
        compiler_params=params(16),
        cost_estimate=pl.CostEstimate(
            flops=8 * group_rows * ff_local,
            bytes_accessed=8 * group_rows * ff_local,
            transcendentals=group_rows * ff_local,
        ),
    )(order, gate_pre, up_pre)
    acts = [act] + [between(act, n) for n in range(1, groups)]

    far, more = lax.optimization_barrier(
        (far, [array[:8, :LANES] for array in [act, *packets[1:]]])
    )
    far_mate = mate(far)
    ready = ready + more
    line_rows = depth * query_count
    total, embed, marks = pl.pallas_call(
        near_kernel,
        out_shape=[
            jax.ShapeDtypeStruct((line_rows, width), jnp.float32),
            jax.ShapeDtypeStruct((line_rows, width), jnp.bfloat16),
            jax.ShapeDtypeStruct((line_rows, LANES), jnp.int32),
        ],
        in_specs=[smem] + [vmem] * (3 + depth),
        out_specs=[vmem] * 3,
        compiler_params=params(16),
        cost_estimate=pl.CostEstimate(
            flops=12 * line_rows * block_labels * width,
            bytes_accessed=6 * block_labels * width,
            transcendentals=0,
        ),
    )(place, label_rows, near, near_mate, *packets)
    parts = pl.pallas_call(
        functools.partial(far_kernel, depth),
        out_shape=[jax.ShapeDtypeStruct((query_count, width), jnp.bfloat16)] * depth,
        in_specs=[smem] + [vmem] * 5 + [anywhere] * len(ready),
        out_specs=[vmem] * depth,
        compiler_params=params(16),
    )(place, far, far_mate, total, embed, marks, *ready)
    resid_bf, resid_again = pl.pallas_call(
        resid_kernel,
        out_shape=[jax.ShapeDtypeStruct((query_count, width), jnp.bfloat16)] * 2,
        in_specs=[vmem, vmem, anywhere] + [vmem] * depth,
        out_specs=[vmem] * 2,
        compiler_params=params(16),
    )(
        final_hidden[0],
        norm_gain,
        weights[-1],
        parts[0],
        *[swap(parts[s], PLANE * s, PLANE * s) for s in range(1, depth)],
    )

    slab = width // groups
    own = jnp.stack(
        [
            lax.dynamic_slice_in_dim(resid_again, ((core - n) % groups) * slab, slab, 1)
            for n in range(groups)
        ]
    )
    line = along(own)
    rows = []
    for some in [line[:1], line[1 : depth // 2 + 1]] + [[piece] for piece in line[depth // 2 + 1 :]]:
        some = jnp.concatenate(some, axis=1)
        first, second = swap(some, 1, 2), swap(some, 2, 1)
        found = (some, first, second, swap(first, 2, 1))
        for start in range(0, some.shape[1], query_count):
            rows.append(
                jnp.concatenate([part[:, start : start + query_count] for part in found], axis=1)
            )
    early = jnp.concatenate(rows[: depth // 2], axis=1)
    late = jnp.concatenate(rows[depth // 2 :], axis=1)
    grads = jnp.concatenate([early, late], axis=1)
    slabs = [grads[0]] + [
        jnp.concatenate([between(half[groups - n], n) for half in (early, late)], axis=0)
        for n in range(1, groups)
    ]

    hidden_grad = pl.pallas_call(
        functools.partial(hidden_kernel, groups),
        out_shape=jax.ShapeDtypeStruct((group_rows, ff_local), jnp.float32),
        in_specs=[vmem] * (1 + groups),
        out_specs=vmem,
        compiler_params=params(16),
        cost_estimate=pl.CostEstimate(
            flops=2 * group_rows * width * ff_local,
            bytes_accessed=2 * ff_local * width,
            transcendentals=0,
        ),
    )(grads, *weights)
    down_grad, gate_grad, up_grad = pl.pallas_call(
        functools.partial(last_kernel, groups),
        out_shape=[jax.ShapeDtypeStruct((ff_local, slab), jnp.float32)]
        + [jax.ShapeDtypeStruct(gate_pre.shape, jnp.bfloat16)] * 2,
        in_specs=[smem] + [vmem] * (3 + 2 * groups),
        out_specs=[anywhere] * 3,
        scratch_shapes=[pltpu.VMEM(gate_pre.shape, jnp.bfloat16)] * 2
        + [
            pltpu.VMEM((ff_local, slab), jnp.float32),
            pltpu.SemaphoreType.DMA((len(pieces(ff_local)) + 2,)),
        ],
        compiler_params=params(20),
        cost_estimate=pl.CostEstimate(
            flops=2 * group_rows * width * ff_local,
            bytes_accessed=4 * ff_local * slab + 8 * group_rows * ff_local,
            transcendentals=group_rows * ff_local,
        ),
    )(order, hidden_grad, gate_pre, up_pre, *acts, *slabs)
    return (resid_bf[None], down_grad.T, gate_grad, up_grad)


def solution(mesh):
    placed = (
        P("label", "fsdp", None),
        P(),
        P("label", None, None),
        P("label", "fsdp", None),
        P("label", "fsdp", None),
        P(None, "fsdp", "label"),
        P(None, "fsdp", "label"),
        P("fsdp", "label"),
    )
    return jax.shard_map(
        shards,
        mesh=mesh,
        in_specs=placed,
        out_specs=(
            P("label", "fsdp", None),
            P("fsdp", "label"),
            P(None, "fsdp", "label"),
            P(None, "fsdp", "label"),
        ),
        check_vma=False,
    )
```

```python
import functools

import jax
import jax.numpy as jnp
from jax import lax
from jax.experimental import pallas as pl
from jax.experimental.pallas import tpu as pltpu
from jax.sharding import PartitionSpec as P

ACTIVE = 8
LBLOCK = 128
QBLOCK = 2
PLANE = 4
LANES = 128
FF_BLOCK = 256
COLUMNS = 512

norm_epsilon = 1e-06


def packet_kernel(hidden, gain, blocks, codes, packet):
    width = hidden.shape[1]
    rows = hidden[...].astype(jnp.float32)
    scale = lax.rsqrt(jnp.mean(rows * rows, axis=1, keepdims=True) + norm_epsilon)
    packet[:, :width] = (rows * scale * gain[...][None]).astype(jnp.bfloat16)

    def ones(shape, hit):
        at = [lax.broadcasted_iota(jnp.int32, shape, d) for d in range(2)]
        return hit(*at).astype(jnp.bfloat16)

    def times(left, right):
        return jnp.dot(left, right, preferred_element_type=jnp.float32)

    block_of = ones((rows.shape[0], blocks.shape[0]), lambda r, c: r // QBLOCK == c)
    owners = times(block_of, blocks[...].astype(jnp.bfloat16)).astype(jnp.bfloat16)
    found = codes[...]
    high = (found // LBLOCK).astype(jnp.bfloat16)
    low = (found % LBLOCK).astype(jnp.bfloat16)
    def spot(n):
        return ones((ACTIVE, LANES), lambda r, c: c == r + n * ACTIVE)

    marks = times(owners, spot(0)) + sum(
        lax.dot_general(
            values, spot(n + 1), (((0,), (0,)), ((), ())), preferred_element_type=jnp.float32
        )
        for n, values in enumerate((high, low))
    )
    packet[:, width:] = marks.astype(jnp.bfloat16)


def slopes(embed, marks, rows, owner, first_label):
    scores = lax.dot_general(
        embed, rows, (((1,), (1,)), ((), ())), preferred_element_type=jnp.float32
    )
    slot = sum(
        jnp.where(marks[:, k : k + 1] == owner, k + 1, 0) for k in range(ACTIVE)
    )
    codes = marks[:, ACTIVE : 2 * ACTIVE] * LBLOCK + marks[:, 2 * ACTIVE : 3 * ACTIVE]
    label = lax.broadcasted_iota(jnp.int32, scores.shape, 1) + first_label
    code = (slot - 1) * LBLOCK + label
    positive = codes[:, 0:1] == code
    for k in range(1, ACTIVE):
        positive |= codes[:, k : k + 1] == code
    target_sign = jnp.where(positive, 1.0, -1.0)
    margin = jnp.maximum(1.0 - target_sign * scores, 0.0)
    return jnp.where(slot > 0, -2.0 * target_sign * margin, 0.0).astype(jnp.bfloat16)


def unpack(packets, width):
    embed = jnp.concatenate([packet[:, :width] for packet in packets], axis=0)
    marks = jnp.concatenate([packet[:, width:] for packet in packets], axis=0)
    return embed, marks.astype(jnp.int32)


def near_kernel(place, own, near, across, *refs):
    packets, (total, embed_out, marks_out) = refs[:-3], refs[-3:]
    width = own.shape[1]
    embed, marks = unpack(packets, width)
    embed_out[...] = embed
    marks_out[...] = marks
    here, parity = place[0], place[1]
    fetched = ((own, here), (near, here ^ (1 + parity)), (across, here ^ (2 - parity)))
    found = [(slopes(embed, marks, rows[...], owner, 0), rows) for rows, owner in fetched]
    for start in range(0, width, COLUMNS):
        span = slice(start, min(start + COLUMNS, width))
        total[:, span] = sum(
            jnp.dot(slope, rows[:, span], preferred_element_type=jnp.float32)
            for slope, rows in found
        )


def far_kernel(depth, place, far, across, total, embed, marks, *refs):
    parts = refs[-depth:]
    width = far.shape[1]
    share = far.shape[0]
    embed, marks = embed[...], marks[...]
    here, parity = place[0], place[1]
    found = [
        slopes(embed, marks, far[...], here ^ 3, parity * share),
        slopes(embed, marks, across[...], here ^ 3, (1 - parity) * share),
    ]
    for start in range(0, width, COLUMNS):
        span = slice(start, min(start + COLUMNS, width))
        added = total[:, span] + sum(
            jnp.dot(slope, rows[:, span], preferred_element_type=jnp.float32)
            for slope, rows in zip(found, (far, across))
        )
        rows = parts[0].shape[0]
        for s, part in enumerate(parts):
            part[:, span] = added[s * rows : (s + 1) * rows].astype(jnp.bfloat16)


def resid_kernel(hidden, gain, ready, *refs):
    parts, out, again = refs[:-2], refs[-2], refs[-1]
    rows = hidden[...].astype(jnp.float32)
    scale = lax.rsqrt(jnp.mean(rows * rows, axis=1, keepdims=True) + norm_epsilon)
    normed = rows * scale
    scaled = gain[...][None] * sum(part[...].astype(jnp.float32) for part in parts)
    out[...] = (
        scale * (scaled - normed * jnp.mean(normed * scaled, axis=1, keepdims=True))
    ).astype(jnp.bfloat16)
    again[...] = out[...]


def pieces(extent):
    return [(start, min(start + FF_BLOCK, extent)) for start in range(0, extent, FF_BLOCK)]


def hold_kernel(*refs):
    sems, half = refs[-1], len(refs) // 2
    copies = [
        pltpu.make_async_copy(refs[n], refs[half + n], sems.at[n]) for n in range(half)
    ]
    for copy in copies:
        copy.start()
    for copy in copies:
        copy.wait()


def act_kernel(order, gate, up, act, rows_held):
    rows = gate.shape[1]
    for i in range(gate.shape[0]):
        gate_full = gate[order[i]].astype(jnp.float32)
        up_full = up[order[i]].astype(jnp.float32)
        rows_held[i * rows : (i + 1) * rows] = gate_full * jax.nn.sigmoid(gate_full) * up_full
    for start, stop in pieces(rows_held.shape[1]):
        act[start:stop] = rows_held[:, start:stop].T.astype(jnp.bfloat16)


def hidden_kernel(groups, grads, *refs):
    weights, hidden_grad = refs[:groups], refs[groups]
    for start, stop in pieces(hidden_grad.shape[1]):
        hidden_grad[:, start:stop] = sum(
            lax.dot_general(
                grads[n],
                weights[n][start:stop],
                (((1,), (1,)), ((), ())),
                preferred_element_type=jnp.float32,
            )
            for n in range(groups)
        )


def last_kernel(groups, order, hidden_grad, gate, up, *refs):
    acts, slabs, refs = refs[:groups], refs[groups : 2 * groups], refs[2 * groups :]
    down_grad, gate_grad, up_grad, gate_held, up_held, held, sems = refs
    spans = pieces(held.shape[0])
    rows, blocks = gate.shape[1], gate.shape[0]
    copies = []
    for n, (start, stop) in enumerate(spans):
        held[start:stop] = sum(
            jnp.dot(act[start:stop], slab[...], preferred_element_type=jnp.float32)
            for act, slab in zip(acts, slabs)
        )
        copies.append(
            pltpu.make_async_copy(held.at[start:stop], down_grad.at[start:stop], sems.at[n])
        )
        copies[-1].start()
        turns = max(1, len(spans) - 1)
        for i in range(n * blocks // turns, min(blocks, (n + 1) * blocks // turns)):
            block = order[i]
            part = hidden_grad[i * rows : (i + 1) * rows]
            gate_full = gate[block].astype(jnp.float32)
            up_full = up[block].astype(jnp.float32)
            sigma = jax.nn.sigmoid(gate_full)
            up_held[block] = (part * gate_full * sigma).astype(jnp.bfloat16)
            gate_held[block] = (
                part * up_full * sigma * (1.0 + gate_full * (1.0 - sigma))
            ).astype(jnp.bfloat16)
        if n == turns - 1:
            copies.append(pltpu.make_async_copy(gate_held, gate_grad, sems.at[len(spans)]))
            copies.append(pltpu.make_async_copy(up_held, up_grad, sems.at[len(spans) + 1]))
            copies[-2].start()
            copies[-1].start()
    for copy in copies:
        copy.wait()


def params(megabytes):
    return pltpu.CompilerParams(vmem_limit_bytes=megabytes * 2**20)


def shards(
    final_hidden, norm_gain, label_weights, active_blocks, positives, gate_pre, up_pre, down_weight
):
    owners = lax.axis_size("label")
    groups = lax.axis_size("fsdp")
    depth = owners // PLANE
    here = lax.axis_index("label")
    core = lax.axis_index("fsdp")
    parity = core % 2
    label_rows = label_weights[0]
    block_labels, width = label_rows.shape
    share = block_labels // 2
    smem = pl.BlockSpec(memory_space=pltpu.SMEM)
    vmem = pl.BlockSpec(memory_space=pltpu.VMEM)
    anywhere = pl.BlockSpec(memory_space=pl.ANY)

    def swap(array, even, odd):
        pairs = [
            (i * groups + f, (i ^ (odd if f % 2 else even)) * groups + f)
            for i in range(owners)
            for f in range(groups)
        ]
        return lax.ppermute(array, ("label", "fsdp"), pairs)

    def mate(array):
        return lax.ppermute(array, "fsdp", [(f, f ^ 1) for f in range(groups)])

    def between(array, step):
        return lax.ppermute(array, "fsdp", [(i, (i + step) % groups) for i in range(groups)])

    query_count = final_hidden.shape[1]
    packet = pl.pallas_call(
        packet_kernel,
        out_shape=jax.ShapeDtypeStruct((query_count, width + LANES), jnp.bfloat16),
        in_specs=[vmem] * 4,
        out_specs=vmem,
        compiler_params=params(16),
    )(final_hidden[0], norm_gain, active_blocks[0], positives[0].T)

    def along(piece):
        line = [piece]
        for s in range(1, depth):
            step = s & -s
            line.append(swap(line[s - step], PLANE * step, PLANE * step))
        return line

    packets = along(packet)

    near = swap(label_rows, 1, 2)
    near_mate = mate(near)
    passing = jnp.where(parity == 0, near[:share], near[share:])
    passing, ready = lax.optimization_barrier((passing, [packets[depth // 2][:8, :LANES]]))
    far = swap(passing, 2, 1)
    place = jnp.stack([here, parity]).astype(jnp.int32)

    plane_masks = jnp.stack([0 * parity, 1 + parity, 2 - parity, 0 * parity + 3])
    order = here ^ (
        PLANE * jnp.arange(depth, dtype=jnp.int32)[:, None] + plane_masks[None, :]
    ).reshape(owners)
    order = order.astype(jnp.int32)
    group_rows = owners * query_count
    ff_local = gate_pre.shape[2]
    weights = [down_weight.T] + [between(down_weight, n).T for n in range(1, groups)]
    others = pl.pallas_call(
        hold_kernel,
        out_shape=[jax.ShapeDtypeStruct(other.shape, other.dtype) for other in weights[1:]],
        in_specs=[anywhere] * (groups - 1),
        out_specs=[vmem] * (groups - 1),
        scratch_shapes=[pltpu.SemaphoreType.DMA((groups,))],
        compiler_params=params(16),
        cost_estimate=pl.CostEstimate(
            flops=0, bytes_accessed=4 * ff_local * width, transcendentals=0
        ),
    )(*weights[1:])
    weights = weights[:1] + list(others)
    act = pl.pallas_call(
        act_kernel,
        out_shape=jax.ShapeDtypeStruct((ff_local, group_rows), jnp.bfloat16),
        in_specs=[smem, vmem, vmem],
        out_specs=vmem,
        scratch_shapes=[pltpu.VMEM((group_rows, ff_local), jnp.float32)],
        compiler_params=params(16),
        cost_estimate=pl.CostEstimate(
            flops=8 * group_rows * ff_local,
            bytes_accessed=8 * group_rows * ff_local,
            transcendentals=group_rows * ff_local,
        ),
    )(order, gate_pre, up_pre)
    acts = [act] + [between(act, n) for n in range(1, groups)]

    far, more = lax.optimization_barrier(
        (far, [array[:8, :LANES] for array in [act, packets[1], packets[-1]]])
    )
    far_mate = mate(far)
    ready = ready + more
    line_rows = depth * query_count
    total, embed, marks = pl.pallas_call(
        near_kernel,
        out_shape=[
            jax.ShapeDtypeStruct((line_rows, width), jnp.float32),
            jax.ShapeDtypeStruct((line_rows, width), jnp.bfloat16),
            jax.ShapeDtypeStruct((line_rows, LANES), jnp.int32),
        ],
        in_specs=[smem] + [vmem] * (3 + depth),
        out_specs=[vmem] * 3,
        compiler_params=params(16),
        cost_estimate=pl.CostEstimate(
            flops=12 * line_rows * block_labels * width,
            bytes_accessed=6 * block_labels * width,
            transcendentals=0,
        ),
    )(place, label_rows, near, near_mate, *packets)
    parts = pl.pallas_call(
        functools.partial(far_kernel, depth),
        out_shape=[jax.ShapeDtypeStruct((query_count, width), jnp.bfloat16)] * depth,
        in_specs=[smem] + [vmem] * 5 + [anywhere] * len(ready),
        out_specs=[vmem] * depth,
        compiler_params=params(16),
    )(place, far, far_mate, total, embed, marks, *ready)
    resid_bf, resid_again = pl.pallas_call(
        resid_kernel,
        out_shape=[jax.ShapeDtypeStruct((query_count, width), jnp.bfloat16)] * 2,
        in_specs=[vmem, vmem, anywhere] + [vmem] * depth,
        out_specs=[vmem] * 2,
        compiler_params=params(16),
    )(
        final_hidden[0],
        norm_gain,
        weights[-1],
        parts[0],
        *[swap(parts[s], PLANE * s, PLANE * s) for s in range(1, depth)],
    )

    slab = width // groups
    own = jnp.stack(
        [
            lax.dynamic_slice_in_dim(resid_again, ((core - n) % groups) * slab, slab, 1)
            for n in range(groups)
        ]
    )
    line = along(own)
    rows = []
    for some in [line[:1], line[1 : depth // 2 + 1]] + [[piece] for piece in line[depth // 2 + 1 :]]:
        some = jnp.concatenate(some, axis=1)
        first, second = swap(some, 1, 2), swap(some, 2, 1)
        found = (some, first, second, swap(first, 2, 1))
        for start in range(0, some.shape[1], query_count):
            rows.append(
                jnp.concatenate([part[:, start : start + query_count] for part in found], axis=1)
            )
    early = jnp.concatenate(rows[: depth // 2], axis=1)
    late = jnp.concatenate(rows[depth // 2 :], axis=1)
    grads = jnp.concatenate([early, late], axis=1)
    slabs = [grads[0]] + [
        jnp.concatenate([between(half[groups - n], n) for half in (early, late)], axis=0)
        for n in range(1, groups)
    ]

    hidden_grad = pl.pallas_call(
        functools.partial(hidden_kernel, groups),
        out_shape=jax.ShapeDtypeStruct((group_rows, ff_local), jnp.float32),
        in_specs=[vmem] * (1 + groups),
        out_specs=vmem,
        compiler_params=params(16),
        cost_estimate=pl.CostEstimate(
            flops=2 * group_rows * width * ff_local,
            bytes_accessed=2 * ff_local * width,
            transcendentals=0,
        ),
    )(grads, *weights)
    down_grad, gate_grad, up_grad = pl.pallas_call(
        functools.partial(last_kernel, groups),
        out_shape=[jax.ShapeDtypeStruct((ff_local, slab), jnp.float32)]
        + [jax.ShapeDtypeStruct(gate_pre.shape, jnp.bfloat16)] * 2,
        in_specs=[smem] + [vmem] * (3 + 2 * groups),
        out_specs=[anywhere] * 3,
        scratch_shapes=[pltpu.VMEM(gate_pre.shape, jnp.bfloat16)] * 2
        + [
            pltpu.VMEM((ff_local, slab), jnp.float32),
            pltpu.SemaphoreType.DMA((len(pieces(ff_local)) + 2,)),
        ],
        compiler_params=params(20),
        cost_estimate=pl.CostEstimate(
            flops=2 * group_rows * width * ff_local,
            bytes_accessed=4 * ff_local * slab + 8 * group_rows * ff_local,
            transcendentals=group_rows * ff_local,
        ),
    )(order, hidden_grad, gate_pre, up_pre, *acts, *slabs)
    return (resid_bf[None], down_grad.T, gate_grad, up_grad)


def solution(mesh):
    placed = (
        P("label", "fsdp", None),
        P(),
        P("label", None, None),
        P("label", "fsdp", None),
        P("label", "fsdp", None),
        P(None, "fsdp", "label"),
        P(None, "fsdp", "label"),
        P("fsdp", "label"),
    )
    return jax.shard_map(
        shards,
        mesh=mesh,
        in_specs=placed,
        out_specs=(
            P("label", "fsdp", None),
            P("fsdp", "label"),
            P(None, "fsdp", "label"),
            P(None, "fsdp", "label"),
        ),
        check_vma=False,
    )
```
